256 devices in a mesh: seq: 64 (over y, z, core), head: 4 (over x).
Axes of the slice: x: 4, y: 4, z: 8, core: 2. Of those that a mesh axis runs over, the one named last changes fastest.
Arguments:
- queries: bfloat16 [16384, 4096], P('seq', 'head'), may hold values from -6 to 6
- keys: bfloat16 [16384, 4096], P('seq', 'head'), may hold values from -6 to 6
- values: bfloat16 [16384, 4096], P('seq', 'head'), may hold values from -6 to 6
- gating: int32 [512, 3], P('seq'), may hold values from 0 to 63, as said below
Outputs:
- attended: bfloat16 [16384, 4096], P('seq', 'head')
- gate_scores: float32 [16384, 64], P('seq')
The draws below stay inside these ranges and needn't reach their ends.
Inputs may be any that keep to these rules, and one draw needn't show every extreme that they name: `gating`: an entry of a tile in block b is b itself (no further block) or an earlier block; among all tiles of one block no earlier block is named twice; every block b >= 1 names block 0 and block b - 1 in some of its tiles.
All inputs are finite; a program needn't handle non-finite values.
Results may differ from the reference program's by a relative error of at most 0.0048.
Values may be sent and summed in bfloat16 or wider, within the bound.
No kernel may reach another device: no remote copies, remote signals or barrier semaphores. Data moves between devices by JAX's collectives and lax.ppermute only.
A program may use at most 64 MiB of HBM per device.

```python
import jax
import jax.numpy as jnp
from jax import lax

HEADS = 32
HD = 128
TOK_DEV = 256
QT = 32
TOPK = 3
FEATURES = 4096
NBLOCKS = 64
TOKENS = 16384
N_SEQ = 64


def draw_queries(key, part):
    key = jax.random.fold_in(key, 11)
    base = jnp.clip(jax.random.normal(key, (TOKENS, FEATURES), jnp.float32), -6.0, 6.0)
    return base.astype(jnp.bfloat16)


def draw_keys(key, part):
    key = jax.random.fold_in(key, 13)
    base = jnp.clip(jax.random.normal(key, (TOKENS, FEATURES), jnp.float32), -6.0, 6.0)
    return base.astype(jnp.bfloat16)


def draw_gating(key, part):
    key = jax.random.fold_in(key, 5)
    shuffle_key = jax.random.fold_in(key, 7)
    blocks = TOKENS // TOK_DEV
    picks = TOK_DEV // QT * TOPK
    noise = jax.random.randint(key, (blocks, blocks), 0, 4096)
    later = jnp.arange(blocks, dtype=jnp.int32)[None, :]
    owner = jnp.arange(blocks, dtype=jnp.int32)[:, None]
    favoured = ((later == 0) | (later == owner - 1)).astype(jnp.int32)
    score = (noise + 8192 * favoured) * blocks + later
    earlier = later < owner
    score = jnp.where(earlier, score, -1 - later)
    order = jnp.argsort(-score, axis=1).astype(jnp.int32)
    reach = min(picks - 1, blocks)
    chosen = order[:, :reach]
    chosen = jnp.where(jnp.take_along_axis(jnp.broadcast_to(earlier, (blocks, blocks)), chosen, axis=1), chosen, owner)
    filler = jnp.broadcast_to(owner, (blocks, picks - reach))
    full = jnp.concatenate([chosen, filler], axis=1)
    mixing = jax.random.randint(shuffle_key, (blocks, picks), 0, 1 << 20) * picks + jnp.arange(picks, dtype=jnp.int32)[None, :]
    places = jnp.argsort(mixing, axis=1).astype(jnp.int32)
    full = jnp.take_along_axis(full, places, axis=1)
    return full.reshape(blocks * (picks // TOPK), TOPK).astype(jnp.int32)


def block_scale(own_key, extent, split, low, high):
    level = 1.0
    for axis_at, parts in split:
        heights = jax.random.uniform(jax.random.fold_in(jax.random.fold_in(own_key, 6), axis_at), (parts,), jnp.float32, low / len(split), high / len(split))
        level = level * jnp.repeat(jnp.exp(heights), extent[axis_at] // parts).reshape((-1,) + (1,) * (len(extent) - 1 - axis_at))
    return level


def normal_values(key, dims, width, bound, split=(), held_as=jnp.bfloat16):
    gain = block_scale(key, dims, split, -0.22, 0.18) if split else 1.0
    values = jax.random.normal(key, dims, jnp.float32) * width * gain
    return jnp.minimum(jnp.maximum(values, -bound), bound).astype(held_as)


def setup_inputs(seed: int = 0) -> dict:
    arg_keys = jax.random.split(jax.random.key(seed), 5)
    queries = draw_queries(jax.random.fold_in(arg_keys[4], 71), 0)
    keys = draw_keys(jax.random.fold_in(arg_keys[4], 71), 0)
    values = normal_values(arg_keys[2], (TOKENS, FEATURES), 1.0, 6.0, ((0, 64), (1, 4)))
    gating = draw_gating(jax.random.fold_in(arg_keys[4], 71), 0)
    return dict(queries=queries, keys=keys, values=values, gating=gating)


def attend(query, key_block, value_block, causal):
    scores = jnp.einsum("qhd,khd->hqk", query, key_block) * (HD ** -0.5)
    if causal:
        places = jnp.arange(query.shape[0])
        scores = jnp.where(jnp.arange(key_block.shape[0])[None, None, :] <= places[None, :, None], scores, -jnp.inf)
    top = jnp.max(scores, axis=2, keepdims=True)
    weights = jnp.exp(scores - top)
    total = jnp.sum(weights, axis=2, keepdims=True)
    rounded = lax.optimization_barrier(weights.astype(jnp.bfloat16)).astype(jnp.float32)
    mixed = jnp.einsum("hqk,khd->qhd", rounded, value_block)
    mixed = mixed / jnp.transpose(total, (1, 0, 2))
    spread = jnp.transpose(top + jnp.log(total), (1, 0, 2))[:, :, 0]
    return mixed, spread


def reference(queries, keys, values, gating):
    tiles = TOK_DEV // QT
    all_q = queries.reshape(N_SEQ, TOK_DEV, HEADS, HD)
    all_k = keys.reshape(N_SEQ, TOK_DEV, HEADS, HD)
    all_v = values.reshape(N_SEQ, TOK_DEV, HEADS, HD)
    all_gates = gating.reshape(N_SEQ, tiles, TOPK)
    means = jnp.mean(all_k.astype(jnp.float32), axis=1)

    def one_block(index):
        query = all_q[index].astype(jnp.float32)
        key_block = all_k[index].astype(jnp.float32)
        value_block = all_v[index].astype(jnp.float32)
        gate = jnp.einsum("thd,jhd->tj", query, means, precision=lax.Precision.HIGHEST) / HEADS
        gate = jnp.where(jnp.arange(N_SEQ)[None, :] < index, gate, 0.0)
        own_out, own_lse = attend(query, key_block, value_block, True)
        tile_q = query.reshape(tiles, QT, HEADS, HD)
        outs = [own_out]
        lses = [own_lse]
        for slot in range(TOPK):
            chosen = all_gates[index][:, slot]
            picked_k = all_k[chosen].astype(jnp.float32)
            picked_v = all_v[chosen].astype(jnp.float32)
            part_out, part_lse = jax.vmap(lambda a, b, c: attend(a, b, c, False))(tile_q, picked_k, picked_v)
            part_out = lax.optimization_barrier(part_out.astype(jnp.bfloat16)).astype(jnp.float32)
            live = chosen != index
            part_lse = jnp.where(live[:, None, None], part_lse, -jnp.inf)
            outs.append(part_out.reshape(TOK_DEV, HEADS, HD))
            lses.append(part_lse.reshape(TOK_DEV, HEADS))
        lse_all = jnp.stack(lses)
        out_all = jnp.stack(outs)
        peak = jnp.max(lse_all, axis=0)
        scale = jnp.exp(lse_all - peak[None])
        final = jnp.sum(scale[..., None] * out_all, axis=0) / jnp.sum(scale, axis=0)[..., None]
        return final.reshape(TOK_DEV, HEADS * HD).astype(jnp.bfloat16), gate

    attended, gates = lax.map(one_block, jnp.arange(N_SEQ))
    return attended.reshape(TOKENS, FEATURES), gates.reshape(TOKENS, NBLOCKS)
```

```python
import functools

import jax
import jax.numpy as jnp
from jax import lax
from jax.experimental import pallas as pl
from jax.experimental.pallas import tpu as pltpu
from jax.sharding import PartitionSpec as P

HEADS = 32
HD = 128
QT = 32
TOPK = 3
NY, NZ, NC = 4, 8, 2
NBLK = NY * NZ * NC
ROWS = 256
WIDTH = 1024
LOCAL = WIDTH // HD
TILES = ROWS // QT
EXT = WIDTH + 128
SCALE = HD ** -0.5
OFFSETS = (0, -1, 1, -2, 2, -3, 3, 4)
GROUPS = ((0, 1, 2), (3, 4), (5, 6), (7,))


def at(y, z, c):
    return (y * NZ + z) * NC + c


def moves(dy=0, dz=0, flip=0, only=None):
    pairs = []
    for y in range(NY):
        if not 0 <= y + dy < NY or (only is not None and y not in only):
            continue
        for z in range(NZ):
            for c in range(NC):
                pairs.append((at(y, z, c), at(y + dy, (z + dz) % NZ, c ^ flip)))
    return pairs


def send(x, **kw):
    return lax.ppermute(x, "seq", moves(**kw))


def softmax_parts(scores):
    top = jnp.max(scores, axis=1, keepdims=True)
    weights = jnp.exp(scores - top)
    total = jnp.sum(weights, axis=1, keepdims=True)
    return top, weights, total


def scores_of(q, k):
    return lax.dot_general(
        q, k, (((1,), (1,)), ((), ())), preferred_element_type=jnp.float32
    ) * SCALE


def own_kernel(q_ref, k_ref, v_ref, out_ref, lse_ref):
    row = lax.broadcasted_iota(jnp.int32, (ROWS, ROWS), 0)
    col = lax.broadcasted_iota(jnp.int32, (ROWS, ROWS), 1)
    lane = lax.broadcasted_iota(jnp.int32, (ROWS, 128), 1)
    spread = jnp.zeros((ROWS, 128), jnp.float32)
    for h in range(LOCAL):
        cols = slice(h * HD, (h + 1) * HD)
        scores = jnp.where(col <= row, scores_of(q_ref[:, cols], k_ref[:, cols]), -jnp.inf)
        top, weights, total = softmax_parts(scores)
        mixed = jnp.dot(weights.astype(jnp.bfloat16), v_ref[:, cols], preferred_element_type=jnp.float32)
        out_ref[:, cols] = mixed / total
        spread = jnp.where(lane == h, top + jnp.log(total), spread)
    lse_ref[...] = spread


def chosen_kernel(count, idx_ref, *refs):
    queries, refs = refs[:8], refs[8:]
    keys, refs = refs[:count], refs[count:]
    values, refs = refs[:count], refs[count:]
    outs, picked = refs[:8], refs[8]
    lane = lax.broadcasted_iota(jnp.int32, (ROWS, 128), 1)
    for i in range(count):
        for s in range(8):
            first = pl.multiple_of(idx_ref[s, i] * QT, QT)
            picked[s * QT:(s + 1) * QT, :] = queries[s][pl.ds(first, QT), :]
        spread = jnp.zeros((ROWS, 128), jnp.float32)
        for h in range(LOCAL):
            cols = slice(h * HD, (h + 1) * HD)
            top, weights, total = softmax_parts(scores_of(picked[:, cols], keys[i][:, cols]))
            mixed = jnp.dot(weights.astype(jnp.bfloat16), values[i][:, cols], preferred_element_type=jnp.float32)
            mixed = (mixed / total).astype(jnp.bfloat16)
            for s in range(8):
                outs[s][i * QT:(i + 1) * QT, cols] = mixed[s * QT:(s + 1) * QT]
            spread = jnp.where(lane % 8 == h, top + jnp.log(total), spread)
        high = spread.astype(jnp.bfloat16).astype(jnp.float32)
        rest = spread - high
        middle = rest.astype(jnp.bfloat16).astype(jnp.float32)
        parts = jnp.where(lane < 8, high, jnp.where(lane < 16, middle, rest - middle))
        parts = jnp.where(lane < 24, parts, 0.0).astype(jnp.bfloat16)
        for s in range(8):
            outs[s][i * QT:(i + 1) * QT, WIDTH:] = parts[s * QT:(s + 1) * QT]


def combine_kernel(sel_ref, own_ref, lse_ref, *refs):
    pieces, out_ref, held, sems = refs[:32], refs[32], refs[33], refs[34]
    copies = []
    for g, places in enumerate(GROUPS):
        for s in range(8):
            copies.append(pltpu.make_async_copy(
                pieces[g * 8 + s],
                held.at[pl.ds((s * 8 + places[0]) * QT, len(places) * QT), :],
                sems.at[g * 8 + s],
            ))
    for copy in copies:
        copy.start()
    for copy in copies:
        copy.wait()
    for t in range(TILES):
        rows = slice(t * QT, (t + 1) * QT)
        spreads = [lse_ref[rows, :]]
        firsts = []
        for c in range(TOPK):
            place = sel_ref[t, c]
            first = pl.multiple_of(jnp.maximum(place, 0) * QT, QT)
            firsts.append(first)
            parts = held[pl.ds(first, QT), WIDTH:].astype(jnp.float32)
            spread = parts + pltpu.roll(parts, 120, 1) + pltpu.roll(parts, 112, 1)
            spreads.append(jnp.where(place >= 0, spread, -jnp.inf))
        peak = functools.reduce(jnp.maximum, spreads)
        scales = [jnp.exp(spread - peak) for spread in spreads]
        total = functools.reduce(jnp.add, scales)
        for h in range(LOCAL):
            cols = slice(h * HD, (h + 1) * HD)
            mixed = scales[0][:, h:h + 1] * own_ref[rows, cols]
            for c in range(TOPK):
                mixed += scales[c + 1][:, h:h + 1] * held[pl.ds(firsts[c], QT), cols].astype(jnp.float32)
            out_ref[rows, cols] = (mixed / total[:, h:h + 1]).astype(jnp.bfloat16)


VMEM = pl.BlockSpec(memory_space=pltpu.VMEM)
SMEM = pl.BlockSpec(memory_space=pltpu.SMEM)
ANY = pl.BlockSpec(memory_space=pl.ANY)
PARAMS = pltpu.CompilerParams(vmem_limit_bytes=40 * 1024 * 1024)


def cost(blocks, extra=0):
    return pl.CostEstimate(
        flops=blocks * ROWS * ROWS * WIDTH * 4,
        bytes_accessed=blocks * 4 * ROWS * WIDTH * 2 + extra,
        transcendentals=blocks * ROWS * ROWS * LOCAL,
    )


def own_attention(q, k, v):
    return pl.pallas_call(
        own_kernel,
        out_shape=(
            jax.ShapeDtypeStruct((ROWS, WIDTH), jnp.float32),
            jax.ShapeDtypeStruct((ROWS, 128), jnp.float32),
        ),
        in_specs=[VMEM] * 3,
        out_specs=(VMEM, VMEM),
        compiler_params=PARAMS,
        cost_estimate=cost(1),
        name="own_attention",
    )(q, k, v)


def chosen_attention(idx, queries, keys, values):
    count = len(keys)
    return pl.pallas_call(
        functools.partial(chosen_kernel, count),
        out_shape=[jax.ShapeDtypeStruct((count * QT, EXT), jnp.bfloat16)] * 8,
        in_specs=[SMEM] + [VMEM] * (8 + 2 * count),
        out_specs=[VMEM] * 8,
        scratch_shapes=[pltpu.VMEM((ROWS, WIDTH), jnp.bfloat16)],
        compiler_params=PARAMS,
        cost_estimate=cost(count, 8 * ROWS * WIDTH * 2),
        name="chosen_attention",
    )(idx, *queries, *keys, *values)


def combine(sel, own_out, own_lse, pieces):
    return pl.pallas_call(
        combine_kernel,
        out_shape=jax.ShapeDtypeStruct((ROWS, WIDTH), jnp.bfloat16),
        in_specs=[SMEM, VMEM, VMEM] + [ANY] * 32,
        out_specs=VMEM,
        scratch_shapes=[
            pltpu.VMEM((8 * 8 * QT, EXT), jnp.bfloat16),
            pltpu.SemaphoreType.DMA((32,)),
        ],
        compiler_params=PARAMS,
        cost_estimate=pl.CostEstimate(flops=8 * ROWS * WIDTH, bytes_accessed=8 << 20, transcendentals=0),
        name="combine",
    )(sel, own_out, own_lse, *pieces)


def gates(queries, keys, me):
    means = (jnp.sum(keys, axis=0, dtype=jnp.float32) / ROWS).reshape(1, WIDTH)
    for bit in range(6):
        other = lax.ppermute(means, "seq", [(i, i ^ (1 << bit)) for i in range(NBLK)])
        means = jnp.concatenate([means, other], axis=0)
    share = lax.dot_general(
        queries.astype(jnp.float32), means, (((1,), (1,)), ((), ())),
        precision=lax.Precision.HIGHEST, preferred_element_type=jnp.float32,
    )
    for bit in range(2):
        share = share + lax.ppermute(share, "head", [(i, i ^ (1 << bit)) for i in range(4)])
    slots = jnp.arange(NBLK)
    order = (slots[:, None] ^ me) == slots[None, :]
    total = jnp.dot(share, order.astype(jnp.float32), precision=lax.Precision.HIGHEST)
    return jnp.where(slots[None, :] < me, total / HEADS, 0.0)


def body(queries, keys, values, gating):
    me = lax.axis_index("seq")
    y, z, c = me // (NZ * NC), (me // NC) % NZ, me % NC

    k_right, v_right, k_left, v_left = [keys], [values], [keys], [values]
    for step in range(1, 5):
        k_right.append(send(k_right[-1], dz=1))
        v_left.append(send(v_left[-1], dz=-1))
        if step < 4:
            v_right.append(send(v_right[-1], dz=1))
            k_left.append(send(k_left[-1], dz=-1))
    key_at = {0: keys, 4: k_right[4]}
    value_at = {0: values, 4: v_left[4]}
    for step in range(1, 4):
        key_at[-step], key_at[step] = k_right[step], k_left[step]
        value_at[-step], value_at[step] = v_right[step], v_left[step]

    choices = jnp.zeros((16, WIDTH), jnp.bfloat16).at[:TILES, :TOPK].set(gating.astype(jnp.bfloat16))
    sent = jnp.concatenate([queries, choices], axis=0)
    down1 = send(sent, dy=-1)
    down3 = send(sent, dy=-3)
    down2 = send(down1, dy=-1, only=(1, 2))
    same = [sent, down1, down2, down3]
    sources = same + [send(x, flip=1) for x in same]

    chosen = jnp.stack([x[ROWS:ROWS + TILES, :TOPK] for x in sources]).astype(jnp.int32)
    places = (z + jnp.array(OFFSETS)) % NZ
    blocks = (y * NZ + places) * NC + c
    hits = jnp.any(chosen[:, :, :, None] == blocks, axis=2)
    idx = jnp.max(jnp.where(hits, jnp.arange(TILES)[None, :, None], 0), axis=1).astype(jnp.int32)

    own_out, own_lse = own_attention(queries, keys, values)
    gate_scores = gates(queries, keys, me)

    pieces = []
    for group in GROUPS:
        outs = chosen_attention(
            idx[:, group[0]:group[-1] + 1],
            sources,
            [key_at[OFFSETS[p]] for p in group],
            [value_at[OFFSETS[p]] for p in group],
        )
        for s in range(8):
            flip, up = s // 4, s % 4
            pieces.append(outs[s] if s == 0 else send(outs[s], dy=up, flip=flip))

    block_y, block_z, block_c = gating // (NZ * NC), (gating // NC) % NZ, gating % NC
    source = (c ^ block_c) * 4 + jnp.clip(y - block_y, 0, NY - 1)
    away = (block_z - z) % NZ
    place = jnp.zeros_like(away)
    for p, offset in enumerate(OFFSETS):
        place = jnp.where(away == offset % NZ, p, place)
    sel = jnp.where(gating != me, source * 8 + place, -1).astype(jnp.int32)
    return combine(sel, own_out, own_lse, pieces), gate_scores


def solution(mesh):
    return jax.shard_map(
        body,
        mesh=mesh,
        in_specs=(P("seq", "head"), P("seq", "head"), P("seq", "head"), P("seq", None)),
        out_specs=(P("seq", "head"), P("seq", None)),
        check_vma=False,
    )
```

```python
import functools

import jax
import jax.numpy as jnp
from jax import lax
from jax.experimental import pallas as pl
from jax.experimental.pallas import tpu as pltpu
from jax.sharding import PartitionSpec as P

HEADS = 32
HD = 128
QT = 32
TOPK = 3
NY, NZ, NC = 4, 8, 2
NBLK = NY * NZ * NC
ROWS = 256
WIDTH = 1024
LOCAL = WIDTH // HD
TILES = ROWS // QT
MEANS = 32
EXT = WIDTH + 128
SCALE = HD ** -0.5
PLACES = [(0, 0, 0), (0, 0, 1)]
for hop in (1, 2, 3):
    PLACES += [(hop, 0, 0), (hop, 0, 1), (hop, 1, 1), (hop, 1, 0)]
PLACES += [(4, 0, 0), (4, 1, 1)]
SPANS = ((0, 6), (6, 10), (10, 14), (14, 16))


def at(y, z, c):
    return (y * NZ + z) * NC + c


COLUMNS = [[(y * NZ + z) * NC + c for y in range(NY)] for z in range(NZ) for c in range(NC)]


def send(x, to):
    pairs = []
    for y in range(NY):
        for z in range(NZ):
            for c in range(NC):
                there = to(y, z, c)
                if there is not None and 0 <= there[0] < NY:
                    pairs.append((at(y, z, c), at(there[0], there[1] % NZ, there[2])))
    return lax.ppermute(x, "seq", pairs)


def ring(x):
    return send(x, lambda y, z, c: (y, z + 1 - 2 * c, c))


def swap(x):
    return send(x, lambda y, z, c: (y, z, 1 - c))


def climb(x, steps):
    return send(x, lambda y, z, c: (y + steps, z, c))


def attend(q, k, v, ones, mask=None):
    scores = lax.dot_general(q, k, (((1,), (1,)), ((), ())), preferred_element_type=jnp.float32)
    if mask is not None:
        scores = jnp.where(mask, scores, -jnp.inf)
    top = jnp.max(scores, axis=1, keepdims=True)
    weights = jnp.exp((scores - top) * SCALE).astype(jnp.bfloat16)
    both = jnp.dot(weights, jnp.concatenate([v, ones], axis=1), preferred_element_type=jnp.float32)
    total = both[:, HD:]
    return both[:, :HD] / total, top * SCALE + jnp.log(total)


def own_kernel(q_ref, k_ref, v_ref, out_ref, lse_ref):
    row = lax.broadcasted_iota(jnp.int32, (ROWS, ROWS), 0)
    col = lax.broadcasted_iota(jnp.int32, (ROWS, ROWS), 1)
    lane = lax.broadcasted_iota(jnp.int32, (ROWS, 128), 1)
    ones = jnp.ones((ROWS, HD), jnp.bfloat16)
    lse_ref[...] = jnp.zeros_like(lse_ref)

    @pl.loop(0, LOCAL // 2)
    def _(half):
        for u in range(2):
            h = half * 2 + u
            cols = pl.ds(pl.multiple_of(h * HD, HD), HD)
            mixed, lse = attend(q_ref[:, cols], k_ref[:, cols], v_ref[:, cols], ones, col <= row)
            out_ref[:, cols] = mixed
            lse_ref[...] = jnp.where(lane == h, lse, lse_ref[...])


def chosen_kernel(span, keys_at, values_at, order_ref, idx_ref, q_ref, *refs):
    arrays = max(a for a, _ in values_at) + 1
    blocks, outs = refs[:arrays], refs[arrays:]
    outs = [outs[0].at[s] for s in range(NY)] if len(outs) == 1 else outs
    sides = [order_ref[s] for s in range(NY)]
    rows = NY * QT
    lane = lax.broadcasted_iota(jnp.int32, (rows, 128), 1)
    ones = jnp.ones((ROWS, HD), jnp.bfloat16)
    for i in range(span[1] - span[0]):
        tiles = [
            pl.ds(pl.multiple_of(idx_ref[side, span[0] + i] * QT, QT), QT) for side in sides
        ]
        (ka, kr), (va, vr) = keys_at[i], values_at[i]
        spread = jnp.zeros((rows, 128), jnp.float32)
        for h in range(LOCAL):
            cols = slice(h * HD, (h + 1) * HD)
            q = jnp.concatenate([q_ref[sides[s], tiles[s], cols] for s in range(NY)], axis=0)
            mixed, lse = attend(q, blocks[ka][kr:kr + ROWS, cols], blocks[va][vr:vr + ROWS, cols], ones)
            mixed = mixed.astype(jnp.bfloat16)
            for s in range(NY):
                outs[s][i * QT:(i + 1) * QT, cols] = mixed[s * QT:(s + 1) * QT]
            spread = jnp.where(lane % 8 == h, lse, spread)
        high = spread.astype(jnp.bfloat16).astype(jnp.float32)
        rest = spread - high
        middle = rest.astype(jnp.bfloat16).astype(jnp.float32)
        parts = jnp.where(lane < 8, high, jnp.where(lane < 16, middle, rest - middle))
        parts = jnp.where(lane < 24, parts, 0.0).astype(jnp.bfloat16)
        for s in range(NY):
            outs[s][i * QT:(i + 1) * QT, WIDTH:] = parts[s * QT:(s + 1) * QT]


def combine_kernel(kinds, last, sel_ref, before_ref, lse_ref, *refs):
    count = len(kinds)
    pieces, outs, held, sems = refs[:count], refs[count:-2], refs[-2], refs[-1]

    def fetch(p, n):
        rows = pl.ds(pl.multiple_of(sel_ref[n, 2] * QT, QT), QT)
        piece = pieces[p].at[sel_ref[n, 1], rows, :] if kinds[p] else pieces[p].at[rows, :]
        return pltpu.make_async_copy(piece, held.at[n], sems.at[n])

    def present(n):
        return (sel_ref[n, 0] >= 0) & (sel_ref[n, 0] < count)

    @pl.loop(0, TILES * TOPK)
    def _(n):
        for p in range(count):
            @pl.when(sel_ref[n, 0] == p)
            def _():
                fetch(p, n).start()

        @pl.when(jnp.logical_not(present(n)))
        def _():
            held[n] = jnp.zeros((QT, EXT), jnp.bfloat16)

    @pl.loop(0, TILES * TOPK)
    def _(n):
        for p in range(count):
            @pl.when(sel_ref[n, 0] == p)
            def _():
                fetch(p, n).wait()

    @pl.loop(0, TILES)
    def _(t):
        rows = pl.ds(pl.multiple_of(t * QT, QT), QT)
        here = [present(t * TOPK + c) for c in range(TOPK)]
        some = functools.reduce(jnp.logical_or, here)

        @pl.when(jnp.logical_not(some))
        def _():
            outs[0][rows, :] = before_ref[rows, :].astype(outs[0].dtype)
            if not last:
                outs[1][rows, :] = lse_ref[rows, :]

        @pl.when(some)
        def _():
            spreads = [lse_ref[rows, :]]
            for c in range(TOPK):
                parts = held[t * TOPK + c, :, WIDTH:].astype(jnp.float32)
                spread = parts + pltpu.roll(parts, 120, 1) + pltpu.roll(parts, 112, 1)
                spreads.append(jnp.where(here[c], spread, -jnp.inf))
            peak = functools.reduce(jnp.maximum, spreads)
            scales = [jnp.exp(spread - peak) for spread in spreads]
            total = functools.reduce(jnp.add, scales)
            scales = [scale / total for scale in scales]
            if not last:
                outs[1][rows, :] = peak + jnp.log(total)
            for h in range(LOCAL):
                cols = slice(h * HD, (h + 1) * HD)
                mixed = scales[0][:, h:h + 1] * before_ref[rows, cols]
                for c in range(TOPK):
                    mixed += scales[c + 1][:, h:h + 1] * held[t * TOPK + c, :, cols].astype(jnp.float32)
                outs[0][rows, cols] = mixed.astype(outs[0].dtype)


def gate_kernel(order_ref, q_ref, *refs):
    means, so_far, out_ref = refs[:order_ref.shape[0] // MEANS], refs[order_ref.shape[0] // MEANS:-1], refs[-1]
    share = jnp.concatenate([
        lax.dot_general(q_ref[...], ref[...], (((1,), (1,)), ((), ())), preferred_element_type=jnp.float32)
        for ref in means
    ], axis=1)
    total = jnp.dot(
        share, order_ref[...], precision=lax.Precision.HIGHEST, preferred_element_type=jnp.float32
    ) * (1.0 / HEADS)
    for ref in so_far:
        total += ref[...]
    out_ref[...] = total


VMEM = pl.BlockSpec(memory_space=pltpu.VMEM)
SMEM = pl.BlockSpec(memory_space=pltpu.SMEM)
HBM = pl.BlockSpec(memory_space=pltpu.HBM)
WIDE = pltpu.CompilerParams(vmem_limit_bytes=60 * 1024 * 1024)
PARAMS = pltpu.CompilerParams(vmem_limit_bytes=16 * 1024 * 1024)


COST = pl.CostEstimate(flops=1, bytes_accessed=1, transcendentals=0)


def own_attention(q, k, v):
    return pl.pallas_call(
        own_kernel,
        out_shape=(
            jax.ShapeDtypeStruct((ROWS, WIDTH), jnp.float32),
            jax.ShapeDtypeStruct((ROWS, 128), jnp.float32),
        ),
        in_specs=[VMEM] * 3,
        out_specs=(VMEM, VMEM),
        compiler_params=PARAMS,
        cost_estimate=COST,
        name="own_attention",
    )(q, k, v)


def chosen_attention(order, idx, sources, blocks, span, keys_at, values_at, apart):
    rows = (span[1] - span[0]) * QT
    shapes = [jax.ShapeDtypeStruct((rows, EXT), jnp.bfloat16)] * NY
    return pl.pallas_call(
        functools.partial(chosen_kernel, span, keys_at, values_at),
        out_shape=shapes if apart else jax.ShapeDtypeStruct((NY, rows, EXT), jnp.bfloat16),
        in_specs=[SMEM] * 2 + [VMEM] * (1 + len(blocks)),
        out_specs=[VMEM] * NY if apart else VMEM,
        compiler_params=PARAMS,
        cost_estimate=COST,
        name="chosen_attention",
    )(order, idx, sources, *blocks)


def combine(sel, state, pieces, last):
    small = jax.ShapeDtypeStruct((ROWS, 128), jnp.float32)
    whole = jax.ShapeDtypeStruct((ROWS, WIDTH), jnp.bfloat16 if last else jnp.float32)
    return pl.pallas_call(
        functools.partial(combine_kernel, tuple(x.ndim == 3 for x in pieces), last),
        out_shape=whole if last else (whole, small),
        in_specs=[SMEM, VMEM, VMEM] + [HBM] * len(pieces),
        out_specs=VMEM if last else (VMEM,) * 2,
        scratch_shapes=[
            pltpu.VMEM((TILES * TOPK, QT, EXT), jnp.bfloat16),
            pltpu.SemaphoreType.DMA((TILES * TOPK,)),
        ],
        compiler_params=WIDE,
        cost_estimate=COST,
        name="combine",
    )(sel, *state, *pieces)


def after(x, *others):
    return lax.optimization_barrier((x,) + others)[0] if others else x


def split(x):
    high = lax.reduce_precision(x, 8, 7)
    middle = lax.reduce_precision(x - high, 8, 7)
    return [high, middle, x - high - middle]


def gates(order, queries, carriers, *so_far):
    return pl.pallas_call(
        gate_kernel,
        out_shape=jax.ShapeDtypeStruct((ROWS, NBLK), jnp.float32),
        in_specs=[VMEM] * (2 + len(carriers) + len(so_far)),
        out_specs=VMEM,
        compiler_params=PARAMS,
        cost_estimate=COST,
        name="gate_share",
    )(order, queries, *carriers, *so_far)


def over_heads(share):
    for bits in (1, 2):
        share = share + lax.ppermute(share, "head", [(i, i ^ bits) for i in range(4)])
    return share


def body(queries, keys, values, gating):
    me = lax.axis_index("seq")
    y, z, c = me // (NZ * NC), (me // NC) % NZ, me % NC
    sign = 2 * c - 1

    k_swapped = swap(keys)
    own_k = jnp.concatenate([keys, k_swapped], axis=0)
    own_v = jnp.concatenate([values, swap(values)], axis=0)
    k_hops, v_hops = [own_k, ring(own_k)], [own_v, ring(own_v)]
    own_out, own_lse = own_attention(queries, keys, values)
    mean = after(jnp.sum(own_k.reshape(NC, ROWS, WIDTH), axis=1, dtype=jnp.float32) / ROWS, own_lse)
    means = jnp.concatenate([mean] + [climb(mean, d) for d in (1, 2, 3)], axis=0)
    means = jnp.concatenate(split(means) + [jnp.zeros((8, WIDTH), jnp.float32)], axis=0).astype(jnp.bfloat16)
    m_hops = [means]
    for _ in range(4):
        m_hops.append(ring(m_hops[-1]))

    choices = jnp.zeros((16, WIDTH), jnp.bfloat16).at[:TILES, :TOPK].set(gating.astype(jnp.bfloat16))
    sources = lax.all_gather(
        jnp.concatenate([queries, choices], axis=0), "seq", axis_index_groups=COLUMNS
    )
    chosen = sources[:, ROWS:ROWS + TILES, :TOPK].astype(jnp.int32)
    blocks = jnp.stack([
        (y * NZ + (z + (sign if chain == 0 else -sign) * hop) % NZ) * NC + (c ^ core)
        for hop, chain, core in PLACES
    ])
    hits = jnp.any(chosen[:, :, :, None] == blocks, axis=2)
    idx = jnp.max(jnp.where(hits, jnp.arange(TILES)[None, :, None], 0), axis=1).astype(jnp.int32)

    block_y, block_z, block_c = gating // (NZ * NC), (gating // NC) % NZ, gating % NC
    ahead = (block_z - z) * sign % NZ
    hop = jnp.minimum(ahead, NZ - ahead)
    core = c ^ block_c
    group = jnp.maximum(hop - 1, 0)
    chain = (ahead > 4) | ((ahead == 4) & (core == 1))
    within = jnp.where(hop == 4, core, jnp.where(chain, 3 - core, core) + jnp.where(hop == 1, 2, 0))
    up = jnp.clip(y - block_y, 0, NY - 1)
    kind = jnp.where(group < 2, group, jnp.where(group == 2, 2 + up, 2 + NY))
    sel = jnp.stack([jnp.where(gating != me, kind, -1), jnp.clip(block_y, 0, NY - 1), within], axis=2)
    sel = sel.reshape(TILES * TOPK, 3).astype(jnp.int32)
    late = jnp.concatenate([jnp.where(sel[:, :1] == 2 + NY, 0, -1), sel[:, 1:]], axis=1)

    r = jnp.arange(8 * MEANS)
    down, part, array = (r % 8) // 2, (r % MEANS) // 8, r // MEANS
    far = jnp.where(array > 4, 4 - array, array)
    column = ((y - down) * NZ + (z + sign * far) % NZ) * NC + (c ^ (array > 4) ^ (r % 2))
    column = jnp.where((part < 3) & (down <= y) & (column < me), column, -1)
    order = (column[:, None] == jnp.arange(NBLK)[None, :]).astype(jnp.float32)
    idx = after(idx, sel, late, order)

    k_other, v_other = [None], [None]
    rows_here = jnp.arange(NY, dtype=jnp.int32)
    rows_up = (rows_here + y) % NY

    def swap_hop(hop, *ties):
        k_other.append(swap(after(k_hops[hop], *ties)))
        v_other.append(swap(after(v_hops[hop], *ties)))

    def attend_hop(hop, idx):
        arrays = [k_hops[hop], v_hops[hop], k_other[hop], v_other[hop]]
        if hop == 1:
            arrays = [own_k, own_v] + arrays
        cuts = (0,) if hop == 4 else (0, ROWS)
        keys_at = [(a, cut) for a in range(0, len(arrays), 2) for cut in cuts]
        values_at = [(a + 1, cut) for a, cut in keys_at]
        apart = hop == 3
        return chosen_attention(rows_up if apart else rows_here, idx, sources, arrays, SPANS[hop - 1], keys_at, values_at, apart)

    def back(out):
        return lax.all_to_all(
            out, "seq", split_axis=0, concat_axis=0, tiled=True, axis_index_groups=COLUMNS
        )

    def back_up(outs):
        return [outs[0]] + [climb(outs[d], d) for d in (1, 2, 3)]

    for _ in range(2):
        k_hops.append(ring(k_hops[-1]))
        v_hops.append(ring(after(v_hops[-1], means) if len(v_hops) == 2 else v_hops[-1]))
    k_hops.append(ring(k_hops[3][:ROWS]))
    v_hops.append(ring(v_hops[3][:ROWS]))
    swap_hop(1)
    out1 = attend_hop(1, idx)
    back1 = back(out1)
    swap_hop(2, out1)
    out2 = attend_hop(2, idx)
    back2 = back(out2)
    swap_hop(3, out2, back1, m_hops[1])
    out3 = attend_hop(3, idx)
    back3 = back_up(out3)
    swap_hop(4, m_hops[2], *out3)
    out4 = attend_hop(4, idx)
    back4 = back(out4)
    m_other = swap(jnp.concatenate(m_hops[1:4], axis=0))

    share = gates(order, queries, m_hops + [m_other[i * MEANS:(i + 1) * MEANS] for i in range(3)])
    gate_scores = over_heads(after(share, out4))
    state = combine(sel, (own_out, own_lse), [back1, back2] + back3, False)
    return combine(late, state, [back4], True), gate_scores


def solution(mesh):
    return jax.shard_map(
        body,
        mesh=mesh,
        in_specs=(P("seq", "head"), P("seq", "head"), P("seq", "head"), P("seq", None)),
        out_specs=(P("seq", "head"), P("seq", None)),
        check_vma=False,
    )
```

```python
import functools

import jax
import jax.numpy as jnp
from jax import lax
from jax.experimental import pallas as pl
from jax.experimental.pallas import tpu as pltpu
from jax.sharding import PartitionSpec as P

HEADS = 32
HD = 128
QT = 32
TOPK = 3
NY, NZ, NC = 4, 8, 2
NBLK = NY * NZ * NC
ROWS = 256
WIDTH = 1024
LOCAL = WIDTH // HD
TILES = ROWS // QT
HALF = LOCAL // 2
LANES = HALF * HD
EXT = LANES + 128
MEANS = 32
SCALE = HD ** -0.5
LOG2E = 1.4426950408889634
ABSENT = -1e30
PLACES = [(0, 0, 0), (0, 0, 1)]
for hop in (1, 2, 3):
    PLACES += [(hop, 0, 0), (hop, 0, 1), (hop, 1, 1), (hop, 1, 0)]
PLACES += [(4, 0, 0), (4, 1, 1)]
COLUMNS = [[(y * NZ + z) * NC + c for y in range(NY)] for z in range(NZ) for c in range(NC)]
PLANES = [[(y * NZ + z) * NC + c for z in range(NZ) for c in range(NC)] for y in range(NY)]


def at(y, z, c):
    return (y * NZ + z) * NC + c


def send(x, to):
    pairs = []
    for y in range(NY):
        for z in range(NZ):
            for c in range(NC):
                there = to(y, z, c)
                if 0 <= there[0] < NY:
                    pairs.append((at(y, z, c), at(there[0], there[1] % NZ, there[2])))
    return lax.ppermute(x, "seq", pairs)


def ring(x):
    return send(x, lambda y, z, c: (y, z + 1 - 2 * c, c))


def swap(x):
    return send(x, lambda y, z, c: (y, z, 1 - c))


def climb(x, steps):
    return send(x, lambda y, z, c: (y + steps, z, c))


def attend(q, k, v, ones, mask=None):
    scores = lax.dot_general(q, k, (((1,), (1,)), ((), ())), preferred_element_type=jnp.float32)
    if mask is not None:
        scores = jnp.where(mask, scores, -jnp.inf)
    top = jnp.max(scores, axis=1, keepdims=True)
    weights = jnp.exp2((scores - top) * (SCALE * LOG2E)).astype(jnp.bfloat16)
    both = jnp.dot(weights, jnp.concatenate([v, ones], axis=1), preferred_element_type=jnp.float32)
    return top * SCALE, both[:, :HD], both[:, HD:]


def own_kernel(q_ref, k_ref, v_ref, first_ref, second_ref, lse_ref):
    row = lax.broadcasted_iota(jnp.int32, (ROWS, ROWS), 0)
    col = lax.broadcasted_iota(jnp.int32, (ROWS, ROWS), 1)
    lane = lax.broadcasted_iota(jnp.int32, (ROWS, 128), 1)
    ones = jnp.ones((ROWS, HD), jnp.bfloat16)
    lse_ref[...] = jnp.zeros_like(lse_ref)

    @pl.loop(0, HALF)
    def _(h):
        for half, out_ref in enumerate((first_ref, second_ref)):
            wide = pl.ds(pl.multiple_of((half * HALF + h) * HD, HD), HD)
            top, mixed, total = attend(q_ref[:, wide], k_ref[:, wide], v_ref[:, wide], ones, col <= row)
            out_ref[:, pl.ds(pl.multiple_of(h * HD, HD), HD)] = mixed / total
            lse_ref[...] = jnp.where(lane == half * HALF + h, top + jnp.log(total), lse_ref[...])


def chosen_kernel(half, blocks, y_ref, idx_ref, *refs):
    arrays = max(a for a, _, _ in blocks) + 1
    queries, held, out_ref = refs[:NY], refs[NY:NY + arrays], refs[NY + arrays]
    kv, acc, tops, totals, sems = refs[NY + arrays + 1:]
    copies = []
    for n, (a, index, row) in enumerate(blocks):
        ref = held[a] if index is None else held[a].at[index]
        copies.append(pltpu.make_async_copy(ref.at[pl.ds(row, 2 * ROWS), :], kv.at[n], sems.at[n]))
    for copy in copies:
        copy.start()
    acc[...] = jnp.zeros_like(acc)
    tops[...] = jnp.full_like(tops, ABSENT)
    totals[...] = jnp.zeros_like(totals)
    ones = jnp.ones((ROWS, HD), jnp.bfloat16)

    @pl.loop(0, len(blocks) // 4)
    def _(some):
        for u in range(4):
            n = some * 4 + u
            pltpu.make_async_copy(kv.at[0], kv.at[n], sems.at[n]).wait()
        for u in range(4):
            n = some * 4 + u
            tiles, present = [], []
            for d in range(NY):
                choice = idx_ref[d, n]
                tiles.append(pl.ds(pl.multiple_of(jnp.maximum(choice, 0) * QT, QT), QT))
                present.append(choice >= 0)
            for h in range(HALF):
                cols = slice(h * HD, (h + 1) * HD)
                wide = slice(half * LANES + h * HD, half * LANES + (h + 1) * HD)
                q = jnp.concatenate([queries[d][tiles[d], wide] for d in range(NY)], axis=0)
                top, mixed, total = attend(q, kv[n, :ROWS, cols], kv[n, ROWS:, cols], ones)
                for d in range(NY):
                    mine = slice(d * QT, (d + 1) * QT)
                    before = tops[d, h, tiles[d], :]
                    now = jnp.where(present[d], top[mine], ABSENT)
                    peak = jnp.maximum(before, now)
                    old = jnp.exp(before - peak)
                    new = jnp.where(present[d], jnp.exp(now - peak), 0.0)
                    tops[d, h, tiles[d], :] = peak
                    totals[d, h, tiles[d], :] = old * totals[d, h, tiles[d], :] + new * total[mine]
                    acc[d, tiles[d], cols] = old * acc[d, tiles[d], cols] + new * mixed[mine]

    lane = lax.broadcasted_iota(jnp.int32, (ROWS, 128), 1)
    for d in range(NY):
        to = lax.rem(y_ref[0] + d, NY)
        spread = jnp.zeros((ROWS, 128), jnp.float32)
        for h in range(HALF):
            cols = slice(h * HD, (h + 1) * HD)
            total = totals[d, h]
            any_here = total > 0
            safe = jnp.where(any_here, total, 1.0)
            out_ref[to, :, cols] = (acc[d, :, cols] / safe).astype(jnp.bfloat16)
            lse = jnp.where(any_here, tops[d, h] + jnp.log(safe), ABSENT)
            spread = jnp.where(lane % HALF == h, lse, spread)
        high = spread.astype(jnp.bfloat16).astype(jnp.float32)
        rest = spread - high
        middle = rest.astype(jnp.bfloat16).astype(jnp.float32)
        parts = jnp.where(lane < HALF, high, jnp.where(lane < 2 * HALF, middle, rest - middle))
        parts = jnp.where(lane < 3 * HALF, parts, 0.0).astype(jnp.bfloat16)
        out_ref[to, :, LANES:] = parts


def combine_kernel(half, y_ref, own_ref, lse_ref, pieces_ref, *refs):
    out_ref = refs[-1]
    if half:
        out_ref[:, :LANES] = refs[0][...]

    @pl.loop(0, TILES)
    def _(t):
        rows = pl.ds(pl.multiple_of(t * QT, QT), QT)
        mine = lse_ref[rows, :]
        spreads = [pltpu.roll(mine, 128 - HALF, 1) if half else mine]
        for r in range(NY):
            parts = pieces_ref[r, rows, LANES:].astype(jnp.float32)
            spread = parts + pltpu.roll(parts, 128 - HALF, 1) + pltpu.roll(parts, 128 - 2 * HALF, 1)
            spreads.append(jnp.where(y_ref[0] >= r, spread, ABSENT))
        peak = functools.reduce(jnp.maximum, spreads)
        scales = [jnp.exp(spread - peak) for spread in spreads]
        total = functools.reduce(jnp.add, scales)
        scales = [scale / total for scale in scales]
        for h in range(HALF):
            cols = slice(h * HD, (h + 1) * HD)
            wide = slice(half * LANES + h * HD, half * LANES + (h + 1) * HD)
            mixed = scales[0][:, h:h + 1] * own_ref[rows, cols]
            for r in range(NY):
                mixed += scales[r + 1][:, h:h + 1] * pieces_ref[r, rows, cols].astype(jnp.float32)
            out_ref[rows, wide if half else cols] = mixed.astype(jnp.bfloat16)


def gate_kernel(order_ref, q_ref, means_ref, out_ref):
    share = lax.dot_general(
        q_ref[...], means_ref[...], (((1,), (1,)), ((), ())), preferred_element_type=jnp.float32
    )
    out_ref[...] = jnp.dot(
        share, order_ref[...], precision=lax.Precision.HIGHEST, preferred_element_type=jnp.float32
    ) * (1.0 / HEADS)


VMEM = pl.BlockSpec(memory_space=pltpu.VMEM)
SMEM = pl.BlockSpec(memory_space=pltpu.SMEM)
HBM = pl.BlockSpec(memory_space=pltpu.HBM)
PARAMS = pltpu.CompilerParams(vmem_limit_bytes=24 * 1024 * 1024)
WIDE = pltpu.CompilerParams(vmem_limit_bytes=60 * 1024 * 1024)
COST = pl.CostEstimate(flops=1, bytes_accessed=1, transcendentals=0)


def call(kernel, name, outs, in_specs, scratch=(), params=PARAMS):
    many = isinstance(outs, tuple)
    return pl.pallas_call(
        kernel,
        out_shape=outs,
        in_specs=in_specs,
        out_specs=(VMEM,) * len(outs) if many else VMEM,
        scratch_shapes=scratch,
        compiler_params=params,
        cost_estimate=COST,
        name=name,
    )


def own_attention(q, k, v):
    half = jax.ShapeDtypeStruct((ROWS, LANES), jnp.float32)
    outs = (half, half, jax.ShapeDtypeStruct((ROWS, 128), jnp.float32))
    return call(own_kernel, "own_attention", outs, [VMEM] * 3)(q, k, v)


def chosen_attention(half, here, idx, queries, arrays, blocks):
    return call(
        functools.partial(chosen_kernel, half, blocks),
        "chosen_attention",
        jax.ShapeDtypeStruct((NY, ROWS, EXT), jnp.bfloat16),
        [SMEM] * 2 + [VMEM] * NY + [HBM] * len(arrays),
        [
            pltpu.VMEM((len(blocks), 2 * ROWS, LANES), jnp.bfloat16),
            pltpu.VMEM((NY, ROWS, LANES), jnp.float32),
            pltpu.VMEM((NY, HALF, ROWS, 128), jnp.float32),
            pltpu.VMEM((NY, HALF, ROWS, 128), jnp.float32),
            pltpu.SemaphoreType.DMA((len(blocks),)),
        ],
        WIDE,
    )(here, idx, *queries, *arrays)


def combine(half, here, own_out, own_lse, pieces, *first):
    width = WIDTH if half else LANES
    return call(
        functools.partial(combine_kernel, half),
        "combine",
        jax.ShapeDtypeStruct((ROWS, width), jnp.bfloat16),
        [SMEM] + [VMEM] * (3 + len(first)),
    )(here, own_out, own_lse, pieces, *first)


def after(x, *others):
    return lax.optimization_barrier((x,) + others)[0] if others else x


def split(x):
    high = lax.reduce_precision(x, 8, 7)
    middle = lax.reduce_precision(x - high, 8, 7)
    return [high, middle, x - high - middle]


def over_heads(share):
    for bits in (1, 2):
        share = share + lax.ppermute(share, "head", [(i, i ^ bits) for i in range(4)])
    return share


def back(out):
    return lax.all_to_all(
        out, "seq", split_axis=0, concat_axis=0, tiled=True, axis_index_groups=COLUMNS
    )


def body(queries, keys, values, gating):
    me = lax.axis_index("seq")
    y, z, c = me // (NZ * NC), (me // NC) % NZ, me % NC
    here = y.reshape(1).astype(jnp.int32)
    sign = 2 * c - 1

    second = jnp.concatenate([keys[:, LANES:], values[:, LANES:]], axis=0)
    hops = [jnp.concatenate([second, swap(second)], axis=0)]
    hops += [ring(hops[0])]
    hops += [ring(hops[1])]
    first = jnp.concatenate([keys[:, :LANES], values[:, :LANES]], axis=0)
    gathered = lax.all_gather(first, "seq", axis_index_groups=PLANES)

    choices = jnp.zeros((16, WIDTH), jnp.bfloat16).at[:TILES, :TOPK].set(gating.astype(jnp.bfloat16))
    sent = jnp.concatenate([queries, choices], axis=0)
    sources = [sent] + [climb(sent, -d) for d in (1, 2, 3)]
    chosen = jnp.stack([x[ROWS:ROWS + TILES, :TOPK] for x in sources]).astype(jnp.int32)

    def tiles_of(blocks):
        hits = jnp.any(chosen[:, :, :, None] == blocks, axis=2)
        tile = jnp.max(jnp.where(hits, jnp.arange(TILES)[None, :, None], -1), axis=1)
        owner = me + jnp.arange(NY)[:, None] * (NZ * NC)
        return jnp.where(blocks[None, :] != owner, tile, -1).astype(jnp.int32)

    in_row = y * (NZ * NC) + jnp.arange(NZ * NC)
    in_ring = jnp.stack([
        (y * NZ + (z + (sign if chain == 0 else -sign) * hop) % NZ) * NC + (c ^ core)
        for hop, chain, core in PLACES
    ])
    idx_first, idx_second = tiles_of(in_row), tiles_of(in_ring)

    own_first, own_second, own_lse = own_attention(queries, keys, values)

    hops.append(ring(after(hops[2], own_lse, *sources)))
    mean = jnp.sum(keys, axis=0, dtype=jnp.float32).reshape(1, WIDTH) / ROWS
    means = jnp.concatenate([mean] + [climb(mean, d) for d in (1, 2, 3)], axis=0)
    means = jnp.concatenate(split(means) + [jnp.zeros((MEANS - 3 * NY, WIDTH), jnp.float32)], axis=0).astype(jnp.bfloat16)
    means = lax.all_gather(after(means, gathered), "seq", axis_index_groups=PLANES)
    r = jnp.arange(NZ * NC * MEANS)
    part, down = (r % MEANS) // NY, r % NY
    column = (y - down) * (NZ * NC) + r // MEANS
    column = jnp.where((part < 3) & (down <= y) & (column < me), column, -1)
    order = (column[:, None] == jnp.arange(NBLK)[None, :]).astype(jnp.float32)
    share = call(
        gate_kernel, "gate_share", jax.ShapeDtypeStruct((ROWS, NBLK), jnp.float32), [VMEM] * 3
    )(order, queries, means.reshape(NZ * NC * MEANS, WIDTH))
    gate_scores = over_heads(share)

    out_first = chosen_attention(
        0, here, idx_first, sources, [gathered], [(0, n, 0) for n in range(NZ * NC)]
    )
    back_first = back(out_first)
    hops[3] = after(hops[3], out_first)
    hops.append(ring(hops[3][:2 * ROWS]))
    others = [None] + [swap(x) for x in hops[1:]]
    arrays = [hops[0]] + [x for n in (1, 2, 3, 4) for x in (hops[n], others[n])]
    blocks = [(a, None, row) for a in range(7) for row in (0, 2 * ROWS)] + [(7, None, 0), (8, None, 0)]
    out_second = chosen_attention(1, here, after(idx_second, out_first), sources, arrays, blocks)
    back_second = back(out_second)
    attended = combine(0, here, own_first, own_lse, back_first)
    return combine(1, here, own_second, own_lse, back_second, attended), gate_scores


def solution(mesh):
    return jax.shard_map(
        body,
        mesh=mesh,
        in_specs=(P("seq", "head"), P("seq", "head"), P("seq", "head"), P("seq", None)),
        out_specs=(P("seq", "head"), P("seq", None)),
        check_vma=False,
    )
```

```python
import functools

import jax
import jax.numpy as jnp
from jax import lax
from jax.experimental import pallas as pl
from jax.experimental.pallas import tpu as pltpu
from jax.sharding import PartitionSpec as P

HEADS = 32
HD = 128
QT = 32
TOPK = 3
NY, NZ, NC = 4, 8, 2
NBLK = NY * NZ * NC
ROWS = 256
WIDTH = 1024
LOCAL = WIDTH // HD
TILES = ROWS // QT
HALF = LOCAL // 2
LANES = HALF * HD
EXT = LANES + 128
MEANS = 32
SCALE = HD ** -0.5
LOG2E = 1.4426950408889634
ABSENT = -1e30
PLACES = [(0, 0, 0), (0, 0, 1)]
for hop in (1, 2, 3):
    PLACES += [(hop, 0, 0), (hop, 0, 1), (hop, 1, 1), (hop, 1, 0)]
PLACES += [(4, 0, 0), (4, 1, 1)]
COLUMNS = [[(y * NZ + z) * NC + c for y in range(NY)] for z in range(NZ) for c in range(NC)]
PLANES = [[(y * NZ + z) * NC + c for z in range(NZ) for c in range(NC)] for y in range(NY)]


def at(y, z, c):
    return (y * NZ + z) * NC + c


def send(x, to):
    pairs = []
    for y in range(NY):
        for z in range(NZ):
            for c in range(NC):
                there = to(y, z, c)
                if 0 <= there[0] < NY:
                    pairs.append((at(y, z, c), at(there[0], there[1] % NZ, there[2])))
    return lax.ppermute(x, "seq", pairs)


def ring(x):
    return send(x, lambda y, z, c: (y, z + 1 - 2 * c, c))


def swap(x):
    return send(x, lambda y, z, c: (y, z, 1 - c))


def climb(x, steps):
    return send(x, lambda y, z, c: (y + steps, z, c))


def attend(q, k, v, ones, mask=None):
    scores = lax.dot_general(q, k, (((1,), (1,)), ((), ())), preferred_element_type=jnp.float32)
    if mask is not None:
        scores = jnp.where(mask, scores, -jnp.inf)
    top = jnp.max(scores, axis=1, keepdims=True)
    weights = jnp.exp2((scores - top) * (SCALE * LOG2E)).astype(jnp.bfloat16)
    both = jnp.dot(weights, jnp.concatenate([v, ones], axis=1), preferred_element_type=jnp.float32)
    return top * SCALE, both[:, :HD], both[:, HD:]


def own_kernel(q_ref, k_ref, v_ref, first_ref, second_ref, lse_ref):
    row = lax.broadcasted_iota(jnp.int32, (ROWS, ROWS), 0)
    col = lax.broadcasted_iota(jnp.int32, (ROWS, ROWS), 1)
    lane = lax.broadcasted_iota(jnp.int32, (ROWS, 128), 1)
    ones = jnp.ones((ROWS, HD), jnp.bfloat16)
    lse_ref[...] = jnp.zeros_like(lse_ref)

    @pl.loop(0, HALF)
    def _(h):
        for half, out_ref in enumerate((first_ref, second_ref)):
            wide = pl.ds(pl.multiple_of((half * HALF + h) * HD, HD), HD)
            top, mixed, total = attend(q_ref[:, wide], k_ref[:, wide], v_ref[:, wide], ones, col <= row)
            out_ref[:, pl.ds(pl.multiple_of(h * HD, HD), HD)] = mixed / total
            lse_ref[...] = jnp.where(lane == half * HALF + h, top + jnp.log(total), lse_ref[...])


def chosen_kernel(half, blocks, y_ref, idx_ref, *refs):
    arrays = max(a for a, _, _ in blocks) + 1
    queries, held, out_ref = refs[:NY], refs[NY:NY + arrays], refs[NY + arrays]
    kv, acc, tops, totals, sems = refs[NY + arrays + 1:]
    copies = []
    for n, (a, index, row) in enumerate(blocks):
        ref = held[a] if index is None else held[a].at[index]
        copies.append(pltpu.make_async_copy(ref.at[pl.ds(row, 2 * ROWS), :], kv.at[n], sems.at[n]))
    for copy in copies:
        copy.start()
    acc[...] = jnp.zeros_like(acc)
    tops[...] = jnp.full_like(tops, ABSENT)
    totals[...] = jnp.zeros_like(totals)
    ones = jnp.ones((ROWS, HD), jnp.bfloat16)

    @pl.loop(0, len(blocks) // 4)
    def _(some):
        for u in range(4):
            n = some * 4 + u
            pltpu.make_async_copy(kv.at[0], kv.at[n], sems.at[n]).wait()
        for u in range(4):
            n = some * 4 + u
            tiles, present = [], []
            for d in range(NY):
                choice = idx_ref[d, n]
                tiles.append(pl.ds(pl.multiple_of(jnp.maximum(choice, 0) * QT, QT), QT))
                present.append(choice >= 0)
            for h in range(HALF):
                cols = slice(h * HD, (h + 1) * HD)
                wide = slice(half * LANES + h * HD, half * LANES + (h + 1) * HD)
                q = jnp.concatenate([queries[d][tiles[d], wide] for d in range(NY)], axis=0)
                top, mixed, total = attend(q, kv[n, :ROWS, cols], kv[n, ROWS:, cols], ones)
                for d in range(NY):
                    mine = slice(d * QT, (d + 1) * QT)
                    before = tops[d, h, tiles[d], :]
                    now = jnp.where(present[d], top[mine], ABSENT)
                    peak = jnp.maximum(before, now)
                    old = jnp.exp(before - peak)
                    new = jnp.where(present[d], jnp.exp(now - peak), 0.0)
                    tops[d, h, tiles[d], :] = peak
                    totals[d, h, tiles[d], :] = old * totals[d, h, tiles[d], :] + new * total[mine]
                    acc[d, tiles[d], cols] = old * acc[d, tiles[d], cols] + new * mixed[mine]

    lane = lax.broadcasted_iota(jnp.int32, (ROWS, 128), 1)
    for d in range(NY):
        to = lax.rem(y_ref[0] + d, NY)
        spread = jnp.zeros((ROWS, 128), jnp.float32)
        for h in range(HALF):
            cols = slice(h * HD, (h + 1) * HD)
            total = totals[d, h]
            any_here = total > 0
            safe = jnp.where(any_here, total, 1.0)
            out_ref[to, :, cols] = (acc[d, :, cols] / safe).astype(jnp.bfloat16)
            lse = jnp.where(any_here, tops[d, h] + jnp.log(safe), ABSENT)
            spread = jnp.where(lane % HALF == h, lse, spread)
        high = spread.astype(jnp.bfloat16).astype(jnp.float32)
        rest = spread - high
        middle = rest.astype(jnp.bfloat16).astype(jnp.float32)
        parts = jnp.where(lane < HALF, high, jnp.where(lane < 2 * HALF, middle, rest - middle))
        parts = jnp.where(lane < 3 * HALF, parts, 0.0).astype(jnp.bfloat16)
        out_ref[to, :, LANES:] = parts


def combine_kernel(half, y_ref, own_ref, lse_ref, pieces_ref, *refs):
    out_ref = refs[-1]
    if half:
        out_ref[:, :LANES] = refs[0][...]

    @pl.loop(0, TILES)
    def _(t):
        rows = pl.ds(pl.multiple_of(t * QT, QT), QT)
        mine = lse_ref[rows, :]
        spreads = [pltpu.roll(mine, 128 - HALF, 1) if half else mine]
        for r in range(NY):
            parts = pieces_ref[r, rows, LANES:].astype(jnp.float32)
            spread = parts + pltpu.roll(parts, 128 - HALF, 1) + pltpu.roll(parts, 128 - 2 * HALF, 1)
            spreads.append(jnp.where(y_ref[0] >= r, spread, ABSENT))
        peak = functools.reduce(jnp.maximum, spreads)
        scales = [jnp.exp(spread - peak) for spread in spreads]
        total = functools.reduce(jnp.add, scales)
        scales = [scale / total for scale in scales]
        for h in range(HALF):
            cols = slice(h * HD, (h + 1) * HD)
            wide = slice(half * LANES + h * HD, half * LANES + (h + 1) * HD)
            mixed = scales[0][:, h:h + 1] * own_ref[rows, cols]
            for r in range(NY):
                mixed += scales[r + 1][:, h:h + 1] * pieces_ref[r, rows, cols].astype(jnp.float32)
            out_ref[rows, wide if half else cols] = mixed.astype(jnp.bfloat16)


def gate_kernel(order_ref, q_ref, means_ref, out_ref):
    share = lax.dot_general(
        q_ref[...], means_ref[...], (((1,), (1,)), ((), ())), preferred_element_type=jnp.float32
    )
    out_ref[...] = jnp.dot(
        share, order_ref[...], precision=lax.Precision.HIGHEST, preferred_element_type=jnp.float32
    ) * (1.0 / HEADS)


VMEM = pl.BlockSpec(memory_space=pltpu.VMEM)
SMEM = pl.BlockSpec(memory_space=pltpu.SMEM)
HBM = pl.BlockSpec(memory_space=pltpu.HBM)
PARAMS = pltpu.CompilerParams(vmem_limit_bytes=24 * 1024 * 1024)
WIDE = pltpu.CompilerParams(vmem_limit_bytes=60 * 1024 * 1024)
COST = pl.CostEstimate(flops=1, bytes_accessed=1, transcendentals=0)


def call(kernel, name, outs, in_specs, scratch=(), params=PARAMS):
    many = isinstance(outs, tuple)
    return pl.pallas_call(
        kernel,
        out_shape=outs,
        in_specs=in_specs,
        out_specs=(VMEM,) * len(outs) if many else VMEM,
        scratch_shapes=scratch,
        compiler_params=params,
        cost_estimate=COST,
        name=name,
    )


def own_attention(q, k, v):
    half = jax.ShapeDtypeStruct((ROWS, LANES), jnp.float32)
    outs = (half, half, jax.ShapeDtypeStruct((ROWS, 128), jnp.float32))
    return call(own_kernel, "own_attention", outs, [VMEM] * 3)(q, k, v)


def chosen_attention(half, here, idx, queries, arrays, blocks):
    return call(
        functools.partial(chosen_kernel, half, blocks),
        "chosen_attention",
        jax.ShapeDtypeStruct((NY, ROWS, EXT), jnp.bfloat16),
        [SMEM] * 2 + [VMEM] * NY + [HBM] * len(arrays),
        [
            pltpu.VMEM((len(blocks), 2 * ROWS, LANES), jnp.bfloat16),
            pltpu.VMEM((NY, ROWS, LANES), jnp.float32),
            pltpu.VMEM((NY, HALF, ROWS, 128), jnp.float32),
            pltpu.VMEM((NY, HALF, ROWS, 128), jnp.float32),
            pltpu.SemaphoreType.DMA((len(blocks),)),
        ],
        WIDE,
    )(here, idx, *queries, *arrays)


def combine(half, here, own_out, own_lse, pieces, *first):
    width = WIDTH if half else LANES
    return call(
        functools.partial(combine_kernel, half),
        "combine",
        jax.ShapeDtypeStruct((ROWS, width), jnp.bfloat16),
        [SMEM] + [VMEM] * (3 + len(first)),
    )(here, own_out, own_lse, pieces, *first)


def after(x, *others):
    return lax.optimization_barrier((x,) + others)[0] if others else x


def split(x):
    high = lax.reduce_precision(x, 8, 7)
    middle = lax.reduce_precision(x - high, 8, 7)
    return [high, middle, x - high - middle]


def over_heads(share):
    for bits in (1, 2):
        share = share + lax.ppermute(share, "head", [(i, i ^ bits) for i in range(4)])
    return share


def back(out):
    return lax.all_to_all(
        out, "seq", split_axis=0, concat_axis=0, tiled=True, axis_index_groups=COLUMNS
    )


def body(queries, keys, values, gating):
    me = lax.axis_index("seq")
    y, z, c = me // (NZ * NC), (me // NC) % NZ, me % NC
    here = y.reshape(1).astype(jnp.int32)
    sign = 2 * c - 1

    second = jnp.concatenate([keys[:, LANES:], values[:, LANES:]], axis=0)
    hops = [jnp.concatenate([second, swap(second)], axis=0)]
    hops += [ring(hops[0])]
    hops += [ring(hops[1])]
    first = jnp.concatenate([keys[:, :LANES], values[:, :LANES]], axis=0)
    gathered = lax.all_gather(first, "seq", axis_index_groups=PLANES)

    choices = jnp.zeros((16, WIDTH), jnp.bfloat16).at[:TILES, :TOPK].set(gating.astype(jnp.bfloat16))
    sent = jnp.concatenate([queries, choices], axis=0)
    sources = [sent] + [climb(sent, -d) for d in (1, 2, 3)]
    chosen = jnp.stack([x[ROWS:ROWS + TILES, :TOPK] for x in sources]).astype(jnp.int32)

    def tiles_of(blocks):
        hits = jnp.any(chosen[:, :, :, None] == blocks, axis=2)
        tile = jnp.max(jnp.where(hits, jnp.arange(TILES)[None, :, None], -1), axis=1)
        owner = me + jnp.arange(NY)[:, None] * (NZ * NC)
        return jnp.where(blocks[None, :] != owner, tile, -1).astype(jnp.int32)

    in_row = y * (NZ * NC) + jnp.arange(NZ * NC)
    in_ring = jnp.stack([
        (y * NZ + (z + (sign if chain == 0 else -sign) * hop) % NZ) * NC + (c ^ core)
        for hop, chain, core in PLACES
    ])
    idx_first, idx_second = tiles_of(in_row), tiles_of(in_ring)

    own_first, own_second, own_lse = own_attention(queries, keys, values)

    mean = jnp.sum(keys, axis=0, dtype=jnp.float32).reshape(1, WIDTH) / ROWS
    means = jnp.concatenate([mean] + [climb(mean, d) for d in (1, 2, 3)], axis=0)
    means = jnp.concatenate(split(means) + [jnp.zeros((MEANS - 3 * NY, WIDTH), jnp.float32)], axis=0).astype(jnp.bfloat16)
    ready = after(hops[2], own_lse, means, *sources)
    same, cross = ring(ready[:2 * ROWS]), ring(ready[2 * ROWS:])

    means = lax.all_gather(after(means, gathered), "seq", axis_index_groups=PLANES)
    r = jnp.arange(NZ * NC * MEANS)
    part, down = (r % MEANS) // NY, r % NY
    column = (y - down) * (NZ * NC) + r // MEANS
    column = jnp.where((part < 3) & (down <= y) & (column < me), column, -1)
    order = (column[:, None] == jnp.arange(NBLK)[None, :]).astype(jnp.float32)
    share = call(
        gate_kernel, "gate_share", jax.ShapeDtypeStruct((ROWS, NBLK), jnp.float32), [VMEM] * 3
    )(order, queries, means.reshape(NZ * NC * MEANS, WIDTH))
    gate_scores = over_heads(share)

    out_first = chosen_attention(
        0, here, idx_first, sources, [gathered], [(0, n, 0) for n in range(NZ * NC)]
    )
    back_first = back(out_first)
    same, cross = after(same, out_first), after(cross, out_first)
    last = ring(same)
    before = [swap(after(hops[n], out_first)) for n in (1, 2)]
    arrays = [hops[0], hops[1], before[0], hops[2], before[1]]
    arrays += [same, cross, swap(same), swap(cross), last, swap(last)]
    blocks = [(a, None, row) for a in range(5) for row in (0, 2 * ROWS)] + [(a, None, 0) for a in range(5, 11)]
    out_second = chosen_attention(1, here, after(idx_second, out_first), sources, arrays, blocks)
    back_second = back(out_second)
    attended = combine(0, here, own_first, own_lse, back_first)
    return combine(1, after(here, gate_scores), own_second, own_lse, back_second, attended), gate_scores


def solution(mesh):
    return jax.shard_map(
        body,
        mesh=mesh,
        in_specs=(P("seq", "head"), P("seq", "head"), P("seq", "head"), P("seq", None)),
        out_specs=(P("seq", "head"), P("seq", None)),
        check_vma=False,
    )
```

```python
import functools

import jax
import jax.numpy as jnp
from jax import lax
from jax.experimental import pallas as pl
from jax.experimental.pallas import tpu as pltpu
from jax.sharding import PartitionSpec as P

HEADS = 32
HD = 128
QT = 32
TOPK = 3
NY, NZ, NC = 4, 8, 2
NBLK = NY * NZ * NC
ROWS = 256
WIDTH = 1024
LOCAL = WIDTH // HD
TILES = ROWS // QT
HALF = LOCAL // 2
LANES = HALF * HD
EXT = LANES + 128
MEANS = 32
SCALE = HD ** -0.5
LOG2E = 1.4426950408889634
ABSENT = -1e30
PLACES = [(0, 0, 0), (0, 0, 1)]
for hop in (1, 2, 3):
    PLACES += [(hop, 0, 0), (hop, 0, 1), (hop, 1, 1), (hop, 1, 0)]
PLACES += [(4, 0, 0), (4, 1, 1)]
COLUMNS = [[(y * NZ + z) * NC + c for y in range(NY)] for z in range(NZ) for c in range(NC)]
PLANES = [[(y * NZ + z) * NC + c for z in range(NZ) for c in range(NC)] for y in range(NY)]


def at(y, z, c):
    return (y * NZ + z) * NC + c


def send(x, to):
    pairs = []
    for y in range(NY):
        for z in range(NZ):
            for c in range(NC):
                there = to(y, z, c)
                if 0 <= there[0] < NY:
                    pairs.append((at(y, z, c), at(there[0], there[1] % NZ, there[2])))
    return lax.ppermute(x, "seq", pairs)


def ring(x):
    return send(x, lambda y, z, c: (y, z + 1 - 2 * c, c))


def swap(x):
    return send(x, lambda y, z, c: (y, z, 1 - c))


def climb(x, steps):
    return send(x, lambda y, z, c: (y + steps, z, c))


def attend(q, k, v, ones, mask=None):
    scores = lax.dot_general(q, k, (((1,), (1,)), ((), ())), preferred_element_type=jnp.float32)
    if mask is not None:
        scores = jnp.where(mask, scores, -jnp.inf)
    top = jnp.max(scores, axis=1, keepdims=True)
    weights = jnp.exp2((scores - top) * (SCALE * LOG2E)).astype(jnp.bfloat16)
    both = jnp.dot(weights, jnp.concatenate([v, ones], axis=1), preferred_element_type=jnp.float32)
    return top * SCALE, both[:, :HD], both[:, HD:]


def own_kernel(q_ref, k_ref, v_ref, first_ref, second_ref, lse_ref):
    row = lax.broadcasted_iota(jnp.int32, (ROWS, ROWS), 0)
    col = lax.broadcasted_iota(jnp.int32, (ROWS, ROWS), 1)
    lane = lax.broadcasted_iota(jnp.int32, (ROWS, 128), 1)
    ones = jnp.ones((ROWS, HD), jnp.bfloat16)
    lse_ref[...] = jnp.zeros_like(lse_ref)

    @pl.loop(0, HALF)
    def _(h):
        for half, out_ref in enumerate((first_ref, second_ref)):
            wide = pl.ds(pl.multiple_of((half * HALF + h) * HD, HD), HD)
            top, mixed, total = attend(q_ref[:, wide], k_ref[:, wide], v_ref[:, wide], ones, col <= row)
            out_ref[:, pl.ds(pl.multiple_of(h * HD, HD), HD)] = mixed / total
            lse_ref[...] = jnp.where(lane == half * HALF + h, top + jnp.log(total), lse_ref[...])


def chosen_kernel(half, blocks, y_ref, idx_ref, *refs):
    arrays = max(a for a, _, _ in blocks) + 1
    queries, held, out_ref = refs[:NY], refs[NY:NY + arrays], refs[NY + arrays]
    kv, acc, tops, totals, sems = refs[NY + arrays + 1:]
    copies = []
    for n, (a, index, row) in enumerate(blocks):
        ref = held[a] if index is None else held[a].at[index]
        copies.append(pltpu.make_async_copy(ref.at[pl.ds(row, 2 * ROWS), :], kv.at[n], sems.at[n]))
    for copy in copies:
        copy.start()
    acc[...] = jnp.zeros_like(acc)
    tops[...] = jnp.full_like(tops, ABSENT)
    totals[...] = jnp.zeros_like(totals)
    ones = jnp.ones((ROWS, HD), jnp.bfloat16)

    @pl.loop(0, len(blocks) // 4)
    def _(some):
        for u in range(4):
            n = some * 4 + u
            pltpu.make_async_copy(kv.at[0], kv.at[n], sems.at[n]).wait()
        for u in range(4):
            n = some * 4 + u
            tiles, present = [], []
            for d in range(NY):
                choice = idx_ref[d, n]
                tiles.append(pl.ds(pl.multiple_of(jnp.maximum(choice, 0) * QT, QT), QT))
                present.append(choice >= 0)
            for h in range(HALF):
                cols = slice(h * HD, (h + 1) * HD)
                wide = slice(half * LANES + h * HD, half * LANES + (h + 1) * HD)
                q = jnp.concatenate([queries[d][tiles[d], wide] for d in range(NY)], axis=0)
                top, mixed, total = attend(q, kv[n, :ROWS, cols], kv[n, ROWS:, cols], ones)
                for d in range(NY):
                    mine = slice(d * QT, (d + 1) * QT)
                    before = tops[d, h, tiles[d], :]
                    now = jnp.where(present[d], top[mine], ABSENT)
                    peak = jnp.maximum(before, now)
                    old = jnp.exp(before - peak)
                    new = jnp.where(present[d], jnp.exp(now - peak), 0.0)
                    tops[d, h, tiles[d], :] = peak
                    totals[d, h, tiles[d], :] = old * totals[d, h, tiles[d], :] + new * total[mine]
                    acc[d, tiles[d], cols] = old * acc[d, tiles[d], cols] + new * mixed[mine]

    lane = lax.broadcasted_iota(jnp.int32, (ROWS, 128), 1)
    for d in range(NY):
        to = lax.rem(y_ref[0] + d, NY)
        spread = jnp.zeros((ROWS, 128), jnp.float32)
        for h in range(HALF):
            cols = slice(h * HD, (h + 1) * HD)
            total = totals[d, h]
            any_here = total > 0
            safe = jnp.where(any_here, total, 1.0)
            out_ref[to, :, cols] = (acc[d, :, cols] / safe).astype(jnp.bfloat16)
            lse = jnp.where(any_here, tops[d, h] + jnp.log(safe), ABSENT)
            spread = jnp.where(lane % HALF == h, lse, spread)
        high = spread.astype(jnp.bfloat16).astype(jnp.float32)
        rest = spread - high
        middle = rest.astype(jnp.bfloat16).astype(jnp.float32)
        parts = jnp.where(lane < HALF, high, jnp.where(lane < 2 * HALF, middle, rest - middle))
        parts = jnp.where(lane < 3 * HALF, parts, 0.0).astype(jnp.bfloat16)
        out_ref[to, :, LANES:] = parts


def combine_kernel(half, y_ref, own_ref, lse_ref, pieces_ref, *refs):
    out_ref = refs[-1]
    if half:
        out_ref[:, :LANES] = refs[0][...]

    @pl.loop(0, TILES)
    def _(t):
        rows = pl.ds(pl.multiple_of(t * QT, QT), QT)
        mine = lse_ref[rows, :]
        spreads = [pltpu.roll(mine, 128 - HALF, 1) if half else mine]
        for r in range(NY):
            parts = pieces_ref[r, rows, LANES:].astype(jnp.float32)
            spread = parts + pltpu.roll(parts, 128 - HALF, 1) + pltpu.roll(parts, 128 - 2 * HALF, 1)
            spreads.append(jnp.where(y_ref[0] >= r, spread, ABSENT))
        peak = functools.reduce(jnp.maximum, spreads)
        scales = [jnp.exp(spread - peak) for spread in spreads]
        total = functools.reduce(jnp.add, scales)
        scales = [scale / total for scale in scales]
        for h in range(HALF):
            cols = slice(h * HD, (h + 1) * HD)
            wide = slice(half * LANES + h * HD, half * LANES + (h + 1) * HD)
            mixed = scales[0][:, h:h + 1] * own_ref[rows, cols]
            for r in range(NY):
                mixed += scales[r + 1][:, h:h + 1] * pieces_ref[r, rows, cols].astype(jnp.float32)
            out_ref[rows, wide if half else cols] = mixed.astype(jnp.bfloat16)


def gate_kernel(order_ref, q_ref, means_ref, out_ref):
    share = lax.dot_general(
        q_ref[...], means_ref[...], (((1,), (1,)), ((), ())), preferred_element_type=jnp.float32
    )
    out_ref[...] = jnp.dot(
        share, order_ref[...], precision=lax.Precision.HIGHEST, preferred_element_type=jnp.float32
    ) * (1.0 / HEADS)


VMEM = pl.BlockSpec(memory_space=pltpu.VMEM)
SMEM = pl.BlockSpec(memory_space=pltpu.SMEM)
HBM = pl.BlockSpec(memory_space=pltpu.HBM)
PARAMS = pltpu.CompilerParams(vmem_limit_bytes=24 * 1024 * 1024)
WIDE = pltpu.CompilerParams(vmem_limit_bytes=60 * 1024 * 1024)
COST = pl.CostEstimate(flops=1, bytes_accessed=1, transcendentals=0)


def call(kernel, name, outs, in_specs, scratch=(), params=PARAMS):
    many = isinstance(outs, tuple)
    return pl.pallas_call(
        kernel,
        out_shape=outs,
        in_specs=in_specs,
        out_specs=(VMEM,) * len(outs) if many else VMEM,
        scratch_shapes=scratch,
        compiler_params=params,
        cost_estimate=COST,
        name=name,
    )


def own_attention(q, k, v):
    half = jax.ShapeDtypeStruct((ROWS, LANES), jnp.float32)
    outs = (half, half, jax.ShapeDtypeStruct((ROWS, 128), jnp.float32))
    return call(own_kernel, "own_attention", outs, [VMEM] * 3)(q, k, v)


def chosen_attention(half, here, idx, queries, arrays, blocks):
    return call(
        functools.partial(chosen_kernel, half, blocks),
        "chosen_attention",
        jax.ShapeDtypeStruct((NY, ROWS, EXT), jnp.bfloat16),
        [SMEM] * 2 + [VMEM] * NY + [HBM] * len(arrays),
        [
            pltpu.VMEM((len(blocks), 2 * ROWS, LANES), jnp.bfloat16),
            pltpu.VMEM((NY, ROWS, LANES), jnp.float32),
            pltpu.VMEM((NY, HALF, ROWS, 128), jnp.float32),
            pltpu.VMEM((NY, HALF, ROWS, 128), jnp.float32),
            pltpu.SemaphoreType.DMA((len(blocks),)),
        ],
        WIDE,
    )(here, idx, *queries, *arrays)


def combine(half, here, own_out, own_lse, pieces, *first):
    width = WIDTH if half else LANES
    return call(
        functools.partial(combine_kernel, half),
        "combine",
        jax.ShapeDtypeStruct((ROWS, width), jnp.bfloat16),
        [SMEM] + [VMEM] * (3 + len(first)),
    )(here, own_out, own_lse, pieces, *first)


def after(x, *others):
    return lax.optimization_barrier((x,) + others)[0] if others else x


def split(x):
    high = lax.reduce_precision(x, 8, 7)
    middle = lax.reduce_precision(x - high, 8, 7)
    return [high, middle, x - high - middle]


def over_heads(share):
    for bits in (1, 2):
        share = share + lax.ppermute(share, "head", [(i, i ^ bits) for i in range(4)])
    return share


def back(out):
    return lax.all_to_all(
        out, "seq", split_axis=0, concat_axis=0, tiled=True, axis_index_groups=COLUMNS
    )


def body(queries, keys, values, gating):
    me = lax.axis_index("seq")
    y, z, c = me // (NZ * NC), (me // NC) % NZ, me % NC
    here = y.reshape(1).astype(jnp.int32)
    sign = 2 * c - 1

    first = jnp.concatenate([keys[:, :LANES], values[:, :LANES]], axis=0)
    second = jnp.concatenate([after(keys[:, LANES:], first), values[:, LANES:]], axis=0)
    hops = [jnp.concatenate([second, swap(second)], axis=0)]
    hops += [ring(hops[0])]
    hops += [ring(hops[1])]
    gathered = lax.all_gather(first, "seq", axis_index_groups=PLANES)

    choices = jnp.zeros((16, WIDTH), jnp.bfloat16).at[:TILES, :TOPK].set(gating.astype(jnp.bfloat16))
    sent = jnp.concatenate([queries, choices], axis=0)
    sources = [sent] + [climb(sent, -d) for d in (1, 2, 3)]
    chosen = jnp.stack([x[ROWS:ROWS + TILES, :TOPK] for x in sources]).astype(jnp.int32)

    def tiles_of(blocks):
        hits = jnp.any(chosen[:, :, :, None] == blocks, axis=2)
        tile = jnp.max(jnp.where(hits, jnp.arange(TILES)[None, :, None], -1), axis=1)
        owner = me + jnp.arange(NY)[:, None] * (NZ * NC)
        return jnp.where(blocks[None, :] != owner, tile, -1).astype(jnp.int32)

    in_row = y * (NZ * NC) + jnp.arange(NZ * NC)
    in_ring = jnp.stack([
        (y * NZ + (z + (sign if chain == 0 else -sign) * hop) % NZ) * NC + (c ^ core)
        for hop, chain, core in PLACES
    ])
    idx_first, idx_second = tiles_of(in_row), tiles_of(in_ring)

    own_first, own_second, own_lse = own_attention(queries, keys, values)

    mean = jnp.sum(keys, axis=0, dtype=jnp.float32).reshape(1, WIDTH) / ROWS
    means = jnp.concatenate([mean] + [climb(mean, d) for d in (1, 2, 3)], axis=0)
    means = jnp.concatenate(split(means) + [jnp.zeros((MEANS - 3 * NY, WIDTH), jnp.float32)], axis=0).astype(jnp.bfloat16)
    ready = after(hops[2], own_lse, means, *sources)
    same, cross = ring(ready[:2 * ROWS]), ring(ready[2 * ROWS:])

    means = lax.all_gather(after(means, gathered), "seq", axis_index_groups=PLANES)
    r = jnp.arange(NZ * NC * MEANS)
    part, down = (r % MEANS) // NY, r % NY
    column = (y - down) * (NZ * NC) + r // MEANS
    column = jnp.where((part < 3) & (down <= y) & (column < me), column, -1)
    order = (column[:, None] == jnp.arange(NBLK)[None, :]).astype(jnp.float32)
    share = call(
        gate_kernel, "gate_share", jax.ShapeDtypeStruct((ROWS, NBLK), jnp.float32), [VMEM] * 3
    )(order, queries, means.reshape(NZ * NC * MEANS, WIDTH))
    gate_scores = over_heads(share)

    out_first = chosen_attention(
        0, here, idx_first, sources, [gathered], [(0, n, 0) for n in range(NZ * NC)]
    )
    back_first = back(out_first)
    same, cross = after(same, out_first), after(cross, out_first)
    last = ring(same)
    before = [swap(after(hops[n], out_first)) for n in (1, 2)]
    arrays = [hops[0], hops[1], before[0], hops[2], before[1]]
    arrays += [same, cross, swap(same), swap(cross), last, swap(last)]
    blocks = [(a, None, row) for a in range(5) for row in (0, 2 * ROWS)] + [(a, None, 0) for a in range(5, 11)]
    out_second = chosen_attention(1, here, after(idx_second, out_first), sources, arrays, blocks)
    back_second = back(out_second)
    attended = combine(0, here, own_first, own_lse, back_first)
    return combine(1, after(here, gate_scores), own_second, own_lse, back_second, attended), gate_scores


def solution(mesh):
    return jax.shard_map(
        body,
        mesh=mesh,
        in_specs=(P("seq", "head"), P("seq", "head"), P("seq", "head"), P("seq", None)),
        out_specs=(P("seq", "head"), P("seq", None)),
        check_vma=False,
    )
```

```python
import functools

import jax
import jax.numpy as jnp
from jax import lax
from jax.experimental import pallas as pl
from jax.experimental.pallas import tpu as pltpu
from jax.sharding import PartitionSpec as P

HEADS = 32
HD = 128
QT = 32
TOPK = 3
NY, NZ, NC = 4, 8, 2
NBLK = NY * NZ * NC
ROWS = 256
WIDTH = 1024
LOCAL = WIDTH // HD
TILES = ROWS // QT
HALF = LOCAL // 2
LANES = HALF * HD
EXT = LANES + 128
MEANS = 32
SCALE = HD ** -0.5
LOG2E = 1.4426950408889634
ABSENT = -1e30
PLACES = [(0, 0, 0), (0, 0, 1)]
for hop in (1, 2, 3):
    PLACES += [(hop, 0, 0), (hop, 0, 1), (hop, 1, 1), (hop, 1, 0)]
PLACES += [(4, 0, 0), (4, 1, 1)]
COLUMNS = [[(y * NZ + z) * NC + c for y in range(NY)] for z in range(NZ) for c in range(NC)]
PLANES = [[(y * NZ + z) * NC + c for z in range(NZ) for c in range(NC)] for y in range(NY)]


def at(y, z, c):
    return (y * NZ + z) * NC + c


def send(x, to):
    pairs = []
    for y in range(NY):
        for z in range(NZ):
            for c in range(NC):
                there = to(y, z, c)
                if 0 <= there[0] < NY:
                    pairs.append((at(y, z, c), at(there[0], there[1] % NZ, there[2])))
    return lax.ppermute(x, "seq", pairs)


def ring(x):
    return send(x, lambda y, z, c: (y, z + 1 - 2 * c, c))


def swap(x):
    return send(x, lambda y, z, c: (y, z, 1 - c))


def climb(x, steps):
    return send(x, lambda y, z, c: (y + steps, z, c))


def attend(q, k, v, ones, mask=None):
    scores = lax.dot_general(q, k, (((1,), (1,)), ((), ())), preferred_element_type=jnp.float32)
    if mask is not None:
        scores = jnp.where(mask, scores, -jnp.inf)
    top = jnp.max(scores, axis=1, keepdims=True)
    weights = jnp.exp2((scores - top) * (SCALE * LOG2E)).astype(jnp.bfloat16)
    both = jnp.dot(weights, jnp.concatenate([v, ones], axis=1), preferred_element_type=jnp.float32)
    return top * SCALE, both[:, :HD], both[:, HD:]


def own_kernel(q_ref, k_ref, v_ref, first_ref, second_ref, lse_ref):
    row = lax.broadcasted_iota(jnp.int32, (ROWS, ROWS), 0)
    col = lax.broadcasted_iota(jnp.int32, (ROWS, ROWS), 1)
    lane = lax.broadcasted_iota(jnp.int32, (ROWS, 128), 1)
    ones = jnp.ones((ROWS, HD), jnp.bfloat16)
    lse_ref[...] = jnp.zeros_like(lse_ref)

    @pl.loop(0, HALF)
    def _(h):
        for half, out_ref in enumerate((first_ref, second_ref)):
            wide = pl.ds(pl.multiple_of((half * HALF + h) * HD, HD), HD)
            top, mixed, total = attend(q_ref[:, wide], k_ref[:, wide], v_ref[:, wide], ones, col <= row)
            out_ref[:, pl.ds(pl.multiple_of(h * HD, HD), HD)] = mixed / total
            lse_ref[...] = jnp.where(lane == half * HALF + h, top + jnp.log(total), lse_ref[...])


def chosen_kernel(half, blocks, y_ref, idx_ref, *refs):
    arrays = max(a for a, _, _ in blocks) + 1
    queries, held, out_ref = refs[:NY], refs[NY:NY + arrays], refs[NY + arrays]
    kv, acc, tops, totals, sems = refs[NY + arrays + 1:]
    copies = []
    for n, (a, index, row) in enumerate(blocks):
        ref = held[a] if index is None else held[a].at[index]
        copies.append(pltpu.make_async_copy(ref.at[pl.ds(row, 2 * ROWS), :], kv.at[n], sems.at[n]))
    for copy in copies:
        copy.start()
    acc[...] = jnp.zeros_like(acc)
    tops[...] = jnp.full_like(tops, ABSENT)
    totals[...] = jnp.zeros_like(totals)
    ones = jnp.ones((ROWS, HD), jnp.bfloat16)

    @pl.loop(0, len(blocks) // 4)
    def _(some):
        for u in range(4):
            n = some * 4 + u
            pltpu.make_async_copy(kv.at[0], kv.at[n], sems.at[n]).wait()
        for u in range(4):
            n = some * 4 + u
            tiles, present = [], []
            for d in range(NY):
                choice = idx_ref[d, n]
                tiles.append(pl.ds(pl.multiple_of(jnp.maximum(choice, 0) * QT, QT), QT))
                present.append(choice >= 0)
            for h in range(HALF):
                cols = slice(h * HD, (h + 1) * HD)
                wide = slice(half * LANES + h * HD, half * LANES + (h + 1) * HD)
                q = jnp.concatenate([queries[d][tiles[d], wide] for d in range(NY)], axis=0)
                top, mixed, total = attend(q, kv[n, :ROWS, cols], kv[n, ROWS:, cols], ones)
                for d in range(NY):
                    mine = slice(d * QT, (d + 1) * QT)
                    before = tops[d, h, tiles[d], :]
                    now = jnp.where(present[d], top[mine], ABSENT)
                    peak = jnp.maximum(before, now)
                    old = jnp.exp(before - peak)
                    new = jnp.where(present[d], jnp.exp(now - peak), 0.0)
                    tops[d, h, tiles[d], :] = peak
                    totals[d, h, tiles[d], :] = old * totals[d, h, tiles[d], :] + new * total[mine]
                    acc[d, tiles[d], cols] = old * acc[d, tiles[d], cols] + new * mixed[mine]

    lane = lax.broadcasted_iota(jnp.int32, (ROWS, 128), 1)
    for d in range(NY):
        to = lax.rem(y_ref[0] + d, NY)
        spread = jnp.zeros((ROWS, 128), jnp.float32)
        for h in range(HALF):
            cols = slice(h * HD, (h + 1) * HD)
            total = totals[d, h]
            any_here = total > 0
            safe = jnp.where(any_here, total, 1.0)
            out_ref[to, :, cols] = (acc[d, :, cols] / safe).astype(jnp.bfloat16)
            lse = jnp.where(any_here, tops[d, h] + jnp.log(safe), ABSENT)
            spread = jnp.where(lane % HALF == h, lse, spread)
        high = spread.astype(jnp.bfloat16).astype(jnp.float32)
        rest = spread - high
        middle = rest.astype(jnp.bfloat16).astype(jnp.float32)
        parts = jnp.where(lane < HALF, high, jnp.where(lane < 2 * HALF, middle, rest - middle))
        parts = jnp.where(lane < 3 * HALF, parts, 0.0).astype(jnp.bfloat16)
        out_ref[to, :, LANES:] = parts


def combine_kernel(half, y_ref, own_ref, lse_ref, pieces_ref, *refs):
    out_ref = refs[-1]
    if half:
        out_ref[:, :LANES] = refs[0][...]

    @pl.loop(0, TILES)
    def _(t):
        rows = pl.ds(pl.multiple_of(t * QT, QT), QT)
        mine = lse_ref[rows, :]
        spreads = [pltpu.roll(mine, 128 - HALF, 1) if half else mine]
        for r in range(NY):
            parts = pieces_ref[r, rows, LANES:].astype(jnp.float32)
            spread = parts + pltpu.roll(parts, 128 - HALF, 1) + pltpu.roll(parts, 128 - 2 * HALF, 1)
            spreads.append(jnp.where(y_ref[0] >= r, spread, ABSENT))
        peak = functools.reduce(jnp.maximum, spreads)
        scales = [jnp.exp(spread - peak) for spread in spreads]
        total = functools.reduce(jnp.add, scales)
        scales = [scale / total for scale in scales]
        for h in range(HALF):
            cols = slice(h * HD, (h + 1) * HD)
            wide = slice(half * LANES + h * HD, half * LANES + (h + 1) * HD)
            mixed = scales[0][:, h:h + 1] * own_ref[rows, cols]
            for r in range(NY):
                mixed += scales[r + 1][:, h:h + 1] * pieces_ref[r, rows, cols].astype(jnp.float32)
            out_ref[rows, wide if half else cols] = mixed.astype(jnp.bfloat16)


def gate_kernel(order_ref, q_ref, means_ref, out_ref):
    share = lax.dot_general(
        q_ref[...], means_ref[...], (((1,), (1,)), ((), ())), preferred_element_type=jnp.float32
    )
    out_ref[...] = jnp.dot(
        share, order_ref[...], precision=lax.Precision.HIGHEST, preferred_element_type=jnp.float32
    ) * (1.0 / HEADS)


VMEM = pl.BlockSpec(memory_space=pltpu.VMEM)
SMEM = pl.BlockSpec(memory_space=pltpu.SMEM)
HBM = pl.BlockSpec(memory_space=pltpu.HBM)
PARAMS = pltpu.CompilerParams(vmem_limit_bytes=24 * 1024 * 1024)
WIDE = pltpu.CompilerParams(vmem_limit_bytes=60 * 1024 * 1024)
COST = pl.CostEstimate(flops=1, bytes_accessed=1, transcendentals=0)


def call(kernel, name, outs, in_specs, scratch=(), params=PARAMS):
    many = isinstance(outs, tuple)
    return pl.pallas_call(
        kernel,
        out_shape=outs,
        in_specs=in_specs,
        out_specs=(VMEM,) * len(outs) if many else VMEM,
        scratch_shapes=scratch,
        compiler_params=params,
        cost_estimate=COST,
        name=name,
    )


def own_attention(q, k, v):
    half = jax.ShapeDtypeStruct((ROWS, LANES), jnp.float32)
    outs = (half, half, jax.ShapeDtypeStruct((ROWS, 128), jnp.float32))
    return call(own_kernel, "own_attention", outs, [VMEM] * 3)(q, k, v)


def chosen_attention(half, here, idx, queries, arrays, blocks):
    return call(
        functools.partial(chosen_kernel, half, blocks),
        "chosen_attention",
        jax.ShapeDtypeStruct((NY, ROWS, EXT), jnp.bfloat16),
        [SMEM] * 2 + [VMEM] * NY + [HBM] * len(arrays),
        [
            pltpu.VMEM((len(blocks), 2 * ROWS, LANES), jnp.bfloat16),
            pltpu.VMEM((NY, ROWS, LANES), jnp.float32),
            pltpu.VMEM((NY, HALF, ROWS, 128), jnp.float32),
            pltpu.VMEM((NY, HALF, ROWS, 128), jnp.float32),
            pltpu.SemaphoreType.DMA((len(blocks),)),
        ],
        WIDE,
    )(here, idx, *queries, *arrays)


def combine(half, here, own_out, own_lse, pieces, *first):
    width = WIDTH if half else LANES
    return call(
        functools.partial(combine_kernel, half),
        "combine",
        jax.ShapeDtypeStruct((ROWS, width), jnp.bfloat16),
        [SMEM] + [VMEM] * (3 + len(first)),
    )(here, own_out, own_lse, pieces, *first)


def after(x, *others):
    return lax.optimization_barrier((x,) + others)[0] if others else x


def split(x):
    high = lax.reduce_precision(x, 8, 7)
    middle = lax.reduce_precision(x - high, 8, 7)
    return [high, middle, x - high - middle]


def over_heads(share):
    for bits in (1, 2):
        share = share + lax.ppermute(share, "head", [(i, i ^ bits) for i in range(4)])
    return share


def back(out):
    return lax.all_to_all(
        out, "seq", split_axis=0, concat_axis=0, tiled=True, axis_index_groups=COLUMNS
    )


def body(queries, keys, values, gating):
    me = lax.axis_index("seq")
    y, z, c = me // (NZ * NC), (me // NC) % NZ, me % NC
    here = y.reshape(1).astype(jnp.int32)
    sign = 2 * c - 1

    first = jnp.concatenate([keys[:, :LANES], values[:, :LANES]], axis=0)
    second = jnp.concatenate([after(keys[:, LANES:], first), values[:, LANES:]], axis=0)
    hops = [jnp.concatenate([second, swap(second)], axis=0)]
    hops += [ring(hops[0])]
    hops += [ring(hops[1])]
    gathered = lax.all_gather(first, "seq", axis_index_groups=PLANES)

    choices = jnp.zeros((16, WIDTH), jnp.bfloat16).at[:TILES, :TOPK].set(gating.astype(jnp.bfloat16))
    sent = jnp.concatenate([queries, choices], axis=0)
    sources = [sent] + [climb(sent, -d) for d in (1, 2, 3)]
    chosen = jnp.stack([x[ROWS:ROWS + TILES, :TOPK] for x in sources]).astype(jnp.int32)

    def tiles_of(blocks):
        hits = jnp.any(chosen[:, :, :, None] == blocks, axis=2)
        tile = jnp.max(jnp.where(hits, jnp.arange(TILES)[None, :, None], -1), axis=1)
        owner = me + jnp.arange(NY)[:, None] * (NZ * NC)
        return jnp.where(blocks[None, :] != owner, tile, -1).astype(jnp.int32)

    in_row = y * (NZ * NC) + jnp.arange(NZ * NC)
    in_ring = jnp.stack([
        (y * NZ + (z + (sign if chain == 0 else -sign) * hop) % NZ) * NC + (c ^ core)
        for hop, chain, core in PLACES
    ])
    idx_first, idx_second = tiles_of(in_row), tiles_of(in_ring)

    own_first, own_second, own_lse = own_attention(queries, keys, values)

    mean = jnp.sum(keys, axis=0, dtype=jnp.float32).reshape(1, WIDTH) / ROWS
    means = jnp.concatenate([mean] + [climb(mean, d) for d in (1, 2, 3)], axis=0)
    means = jnp.concatenate(split(means) + [jnp.zeros((MEANS - 3 * NY, WIDTH), jnp.float32)], axis=0).astype(jnp.bfloat16)
    ready = after(hops[2], own_lse, means, idx_first, *sources)
    same, cross = ring(ready[:2 * ROWS]), ring(ready[2 * ROWS:])

    means = lax.all_gather(after(means, gathered), "seq", axis_index_groups=PLANES)
    r = jnp.arange(NZ * NC * MEANS)
    part, down = (r % MEANS) // NY, r % NY
    column = (y - down) * (NZ * NC) + r // MEANS
    column = jnp.where((part < 3) & (down <= y) & (column < me), column, -1)
    order = (column[:, None] == jnp.arange(NBLK)[None, :]).astype(jnp.float32)
    share = call(
        gate_kernel, "gate_share", jax.ShapeDtypeStruct((ROWS, NBLK), jnp.float32), [VMEM] * 3
    )(order, queries, means.reshape(NZ * NC * MEANS, WIDTH))
    gate_scores = over_heads(share)

    out_first = chosen_attention(
        0, here, idx_first, sources, [gathered], [(0, n, 0) for n in range(NZ * NC)]
    )
    back_first = back(out_first)
    same, cross = after(same, out_first), after(cross, out_first)
    last = ring(same)
    before = [swap(after(hops[n], out_first)) for n in (1, 2)]
    arrays = [hops[0], hops[1], before[0], hops[2], before[1]]
    arrays += [same, cross, swap(same), swap(cross), last, swap(last)]
    blocks = [(a, None, row) for a in range(5) for row in (0, 2 * ROWS)] + [(a, None, 0) for a in range(5, 11)]
    out_second = chosen_attention(1, here, after(idx_second, out_first), sources, arrays, blocks)
    back_second = back(out_second)
    attended = combine(0, here, own_first, own_lse, back_first)
    return combine(1, after(here, gate_scores), own_second, own_lse, back_second, attended), gate_scores


def solution(mesh):
    return jax.shard_map(
        body,
        mesh=mesh,
        in_specs=(P("seq", "head"), P("seq", "head"), P("seq", "head"), P("seq", None)),
        out_specs=(P("seq", "head"), P("seq", None)),
        check_vma=False,
    )
```
